32 devices in a mesh: view: 2 (over core), tm: 16 (over z, y, x).
Axes of the slice: x: 2, y: 2, z: 4, core: 2. Of those that a mesh axis runs over, the one named last changes fastest.
Arguments:
- frames_x: bfloat16 [2, 16, 384, 1152], P('view', 'tm'), may hold values from -6 to 6
- box_embed: bfloat16 [2, 16, 16, 1152], P('view', 'tm'), may hold values from -6 to 6
- box_count: int32 [2, 16], P('view', 'tm'), may hold values from 1 to 16
- frame_valid: int32 [2, 16], P('view', 'tm'), may hold values 0 or 1
- cycle_link: int32 [2, 2], P('view'), may hold values 0 or 1
- w_qkv: bfloat16 [1152, 3456], P('tm'), may hold values from -0.47140452 to 0.47140452
- w_out: bfloat16 [1152, 1152], P('tm'), may hold values from -0.1875 to 0.1875
- box_gate: float32 [288], replicated, may hold values from -2 to 2
Outputs:
- mixed: bfloat16 [2, 16, 384, 1152], P('view', 'tm')
The draws below stay inside these ranges and needn't reach their ends.
All inputs are finite; a program needn't handle non-finite values. No bound on the sum of `frame_valid` or of `cycle_link` on one device may be relied on, other than what follows from the above.
Results may differ from the reference program's by a relative error of at most 0.0045.
The reference program's roundings to bfloat16 on the way (of `qkv`, `box_kv` and `attn`) count: a program that leaves them out, or rounds other values in their place, can miss the bound.
Values may be sent and summed in bfloat16 or wider, within the bound.
No kernel may reach another device: no remote copies, remote signals or barrier semaphores. Data moves between devices by JAX's collectives and lax.ppermute only.
A program may use at most 128 MiB of HBM per device.

```python
import jax
import jax.numpy as jnp
from jax import lax

D = 1152
HD = 72
CROSS_HEADS = 8
TIME_HEADS = 4
BOX_HEADS = 4
P_SIZE = 384
NB = 16
NV = 2
FRAMES = 16


def draw_frames_x(key, part):

    def camera_draw(camera):
        camera_key = jax.random.fold_in(jax.random.fold_in(key, 101), camera)
        noise = jax.random.normal(jax.random.fold_in(camera_key, 1), (FRAMES, P_SIZE, D), jnp.float32)
        noise = jnp.clip(noise, -6.0, 6.0)
        return noise.astype(jnp.bfloat16)
    return lax.map(camera_draw, jnp.arange(NV, dtype=jnp.int32))


def draw_w_qkv(key, part):
    base = jax.random.normal(jax.random.fold_in(key, 3), (D, 3 * D), jnp.float32)
    base = jnp.clip(base, -6.0, 6.0) * D ** (-0.5)
    return base.astype(jnp.bfloat16)


def with_ends(values, key, least, high):
    longest = values.shape.index(max(values.shape))
    spots = []
    for shift in (0, 1):
        where = [jax.random.randint(jax.random.fold_in(key, axis), (), 0, length) for axis, length in enumerate(values.shape)]
        where[longest] = (where[longest] + shift) % values.shape[longest]
        spots.append(tuple(where))
    return values.at[spots[0]].set(least).at[spots[1]].set(high)


def levels(key, dims, cuts, smallest, high):
    def one(axis_at, parts):
        heights = jax.random.uniform(jax.random.fold_in(jax.random.fold_in(key, 6), axis_at), (parts,), jnp.float32, smallest / len(cuts), high / len(cuts))
        return jnp.repeat(jnp.exp(heights), dims[axis_at] // parts).reshape((-1,) + (1,) * (len(dims) - axis_at - 1))

    loudness = one(*cuts[0])
    for cut in cuts[1:]:
        loudness = loudness * one(*cut)
    return loudness


def scatter_about(rng, extent, spread, limit, cuts=(), held_as=jnp.bfloat16):
    result = spread * jax.random.normal(rng, extent, jnp.float32)
    if cuts:
        result = result * levels(rng, extent, cuts, -0.22, 0.18)
    return jnp.clip(result, -limit, limit).astype(held_as)


def setup_inputs(seed: int = 0) -> dict:
    arg_keys = jax.random.split(jax.random.key(seed), 9)
    return {
        "frames_x": draw_frames_x(jax.random.fold_in(arg_keys[8], 71), 0),
        "box_embed": scatter_about(arg_keys[1], (NV, FRAMES, NB, D), 1.0, 6.0, ((0, 2), (1, 16))),
        "box_count": with_ends(jax.random.randint(arg_keys[2], (NV, FRAMES), 1, NB + 1), jax.random.fold_in(arg_keys[2], 1), 1, NB).astype(jnp.int32),
        "frame_valid": with_ends((jax.random.randint(arg_keys[3], (NV, FRAMES), 0, 4) < 3).astype(jnp.int32), jax.random.fold_in(arg_keys[3], 1), 0, 1),
        "cycle_link": with_ends((jax.random.randint(arg_keys[4], (NV, 2), 0, 4) < 3).astype(jnp.int32), jax.random.fold_in(arg_keys[4], 1), 0, 1),
        "w_qkv": draw_w_qkv(jax.random.fold_in(arg_keys[8], 71), 0),
        "w_out": scatter_about(arg_keys[6], (D, D), D ** -0.5, 0.1875, ((0, 16),)),
        "box_gate": jnp.clip(jax.random.uniform(arg_keys[7], (BOX_HEADS * HD,), jnp.float32, -2.0, 2.0), -2.0, 2.0),
    }


def attend(queries, key_rows, value_rows, live_mask):
    scale = HD ** -0.5
    scores = jnp.einsum("qhe,khe->hqk", queries.astype(jnp.float32), key_rows.astype(jnp.float32)) * scale
    scores = jnp.where(live_mask[None, None, :] > 0, scores, -1e30)
    row_max = jnp.max(scores, axis=-1, keepdims=True)
    expos = jnp.exp(scores - row_max)
    weights = (expos / jnp.sum(expos, axis=-1, keepdims=True)).astype(jnp.bfloat16)
    return jnp.einsum("hqk,khe->qhe", weights.astype(jnp.float32), value_rows.astype(jnp.float32))


def reference(frames_x, box_embed, box_count, frame_valid, cycle_link, w_qkv, w_out, box_gate):
    cross_width = CROSS_HEADS * HD
    time_width = TIME_HEADS * HD
    box_width = BOX_HEADS * HD

    def project(camera):
        token_rows = camera.reshape(FRAMES * P_SIZE, D)
        product = jnp.dot(token_rows, w_qkv, preferred_element_type=jnp.float32)
        return product.astype(jnp.bfloat16).reshape(FRAMES, P_SIZE, 3 * D)

    qkv = lax.map(project, frames_x)
    box_columns = jnp.concatenate([w_qkv[:, 2 * D - box_width:2 * D], w_qkv[:, 3 * D - box_width:]], axis=1)
    box_kv = jnp.dot(box_embed.reshape(NV * FRAMES * NB, D), box_columns, preferred_element_type=jnp.float32)
    box_kv = box_kv.astype(jnp.bfloat16).reshape(NV, FRAMES * NB, 2 * box_width)
    slot_ids = jnp.arange(NB, dtype=jnp.int32)
    box_live = ((slot_ids[None, None, :] < box_count[:, :, None]) & (frame_valid[:, :, None] == 1))
    box_live = box_live.astype(jnp.float32).reshape(NV, FRAMES * NB)
    cross_keys = qkv[..., D:D + cross_width]
    cross_values = qkv[..., 2 * D:2 * D + cross_width]
    keys_all = jnp.concatenate([jnp.roll(cross_keys, 1, 0), cross_keys, jnp.roll(cross_keys, -1, 0)], axis=2)
    values_all = jnp.concatenate([jnp.roll(cross_values, 1, 0), cross_values, jnp.roll(cross_values, -1, 0)], axis=2)
    all_ones = jnp.ones((P_SIZE,), jnp.float32)
    frame_ones = jnp.ones((FRAMES,), jnp.float32)

    def camera_block(camera_index):
        link_flags = cycle_link[camera_index].astype(jnp.float32)
        cross_live = jnp.concatenate([all_ones * link_flags[0], all_ones, all_ones * link_flags[1]])
        camera_qkv = qkv[camera_index]
        camera_box = box_kv[camera_index]
        box_mask = jnp.concatenate([all_ones, box_live[camera_index]])

        def frame_block(frame_index):
            frame_row = camera_qkv[frame_index]
            cross_query = frame_row[:, :cross_width].reshape(P_SIZE, CROSS_HEADS, HD)
            cross_key = keys_all[camera_index, frame_index].reshape(3 * P_SIZE, CROSS_HEADS, HD)
            cross_value = values_all[camera_index, frame_index].reshape(3 * P_SIZE, CROSS_HEADS, HD)
            cross = attend(cross_query, cross_key, cross_value, cross_live).reshape(P_SIZE, cross_width)
            box_query = frame_row[:, cross_width + time_width:D].reshape(P_SIZE, BOX_HEADS, HD)
            box_key = jnp.concatenate([frame_row[:, 2 * D - box_width:2 * D], camera_box[:, :box_width]], axis=0)
            box_value = jnp.concatenate([frame_row[:, 3 * D - box_width:], camera_box[:, box_width:]], axis=0)
            boxed = attend(box_query, box_key.reshape(-1, BOX_HEADS, HD), box_value.reshape(-1, BOX_HEADS, HD), box_mask)
            boxed = boxed.reshape(P_SIZE, box_width) * jnp.tanh(box_gate)
            return cross, boxed

        cross, boxed = lax.map(frame_block, jnp.arange(FRAMES, dtype=jnp.int32))
        time_query = camera_qkv[..., cross_width:cross_width + time_width].reshape(FRAMES, P_SIZE, TIME_HEADS, HD)
        time_key = camera_qkv[..., D + cross_width:D + cross_width + time_width].reshape(FRAMES, P_SIZE, TIME_HEADS, HD)
        time_value = camera_qkv[..., 2 * D + cross_width:2 * D + cross_width + time_width].reshape(FRAMES, P_SIZE, TIME_HEADS, HD)
        timed = jax.vmap(lambda qq, kk, vv: attend(qq, kk, vv, frame_ones), in_axes=1, out_axes=1)(time_query, time_key, time_value)
        attn = jnp.concatenate([cross, timed.reshape(FRAMES, P_SIZE, time_width), boxed], axis=-1).astype(jnp.bfloat16)
        projected = jnp.dot(attn.reshape(FRAMES * P_SIZE, D), w_out, preferred_element_type=jnp.float32)
        residual = frames_x[camera_index].reshape(FRAMES * P_SIZE, D).astype(jnp.float32)
        return (residual + projected).astype(jnp.bfloat16).reshape(FRAMES, P_SIZE, D)

    return lax.map(camera_block, jnp.arange(NV, dtype=jnp.int32))
```

```python
import functools

import jax
import jax.numpy as jnp
from jax import lax
from jax.experimental import pallas as pl
from jax.experimental.pallas import tpu as pltpu
from jax.sharding import PartitionSpec as P

HD = 72
CROSS_HEADS = 8
TIME_HEADS = 4
BOX_HEADS = 4
DEAD = -1e30
VMEM_BYTES = 50 * 2**20
F32 = jnp.float32
BF16 = jnp.bfloat16


def swap(value, axis, by):
    size = lax.axis_size(axis)
    return lax.ppermute(value, axis, [(i, i ^ by) for i in range(size)])


def gather_blocks(shard, first, second):
    size = lax.axis_size("tm")
    near = jnp.concatenate([shard] + [swap(shard, "tm", d) for d in range(4, size, 4)], axis=0)
    one = swap(near, "tm", first)
    two = swap(jnp.concatenate([near, one], axis=0), "tm", second)
    rows = near.shape[0]
    if first == 1:
        return jnp.concatenate([near, one, two], axis=0)
    return jnp.concatenate([near, two[:rows], one, two[rows:]], axis=0)


def block_order(size):
    far = list(range(0, size, 4))
    return [f ^ low for low in range(4) for f in far]


def dot(a, b):
    return jnp.dot(a, b, preferred_element_type=F32)


def dot_t(a, b):
    return lax.dot_general(a, b, (((1,), (1,)), ((), ())), preferred_element_type=F32)


def chooser(rows, source, offset=0):
    row_ids = lax.broadcasted_iota(jnp.int32, (rows, source.shape[1]), 0)
    return (row_ids + offset == source).astype(F32).astype(BF16)


def attend_heads(query, keys, values, score_edits, weight_edits, acc_ref):
    width = query.shape[1]
    scale = HD ** (-0.5)
    for head in range(width // HD):
        low, high = head * HD, (head + 1) * HD
        left = low // 128 * 128
        right = min(width, -(-high // 128) * 128)
        lane = lax.broadcasted_iota(jnp.int32, (1, right - left), 1) + left
        mine = (lane >= low) & (lane < high)
        q = jnp.where(mine, query[:, left:right].astype(F32), 0.0).astype(BF16)
        scores = [edit(dot_t(q, k[:, left:right]) * scale) for k, edit in zip(keys, score_edits)]
        top = functools.reduce(
            jnp.maximum, [jnp.max(s, axis=-1, keepdims=True) for s in scores]
        )
        expos = [edit(jnp.exp(s - top)) for s, edit in zip(scores, weight_edits)]
        total = sum(jnp.sum(e, axis=-1, keepdims=True) for e in expos)
        out = sum(dot(e.astype(BF16), v[:, left:right]) for e, v in zip(expos, values))
        out = out / total
        acc_ref[:, left:right] = jnp.where(mine, out, acc_ref[:, left:right])


def same(x):
    return x


def order_kernel(tokens_ref, *refs, others):
    other_refs = refs[:others]
    source_ref, wide_source_ref, out_ref, wide_ref = refs[others : others + 4]
    out_refs = refs[others + 4 :]
    depth = tokens_ref.shape[1]
    pick = chooser(depth, source_ref[...])
    out_ref[...] = dot(tokens_ref[...], pick).astype(BF16)
    for a, b in zip(other_refs, out_refs):
        b[...] = dot(a[...], pick).astype(BF16)
    wide_ref[...] = dot(tokens_ref[...], chooser(depth, wide_source_ref[...])).astype(BF16)


def time_kernel(tokens_ref, source_ref, mine_ref, theirs_ref, out_ref, acc_ref, *, positions):
    rows, depth = tokens_ref.shape
    part = out_ref.shape[1] // 2
    tokens = dot(tokens_ref[...], chooser(depth, source_ref[...])).astype(BF16)
    place = lax.rem(lax.broadcasted_iota(jnp.int32, (rows, 1), 0), positions)
    place_t = lax.rem(lax.broadcasted_iota(jnp.int32, (1, rows), 1), positions)
    live = place == place_t
    for half, ref in enumerate((mine_ref, theirs_ref)):
        qkv = dot(tokens, ref[...]).astype(BF16)
        attend_heads(
            qkv[:, :part],
            [qkv[:, part : 2 * part]],
            [qkv[:, 2 * part : 3 * part]],
            [lambda s: jnp.where(live, s, DEAD)],
            [same],
            acc_ref,
        )
        out_ref[:, half * part : (half + 1) * part] = acc_ref[...].astype(BF16)


def box_kernel(
    tokens_ref, wide_ref, source_ref, gate_ref, first_mine, first_theirs, mine_ref, theirs_ref,
    out_ref, acc_ref, box_ref, *, slots, blocks,
):
    rows, depth = tokens_ref.shape
    part = out_ref.shape[1] // 2
    fold = mine_ref.shape[1]
    folds = depth // fold
    block = mine_ref.shape[0] // blocks
    lane = lax.broadcasted_iota(jnp.int32, (1, blocks * slots), 1)
    live = jnp.zeros((1, blocks * slots), F32)
    repeats = -(-blocks * slots // fold)
    for b in range(blocks):
        for j in range(folds):
            box_ref[b * slots : (b + 1) * slots, j * fold : (j + 1) * fold] = mine_ref[
                b * block + j * slots : b * block + (j + 1) * slots, :
            ]
        at = b * block + folds * slots
        flags = mine_ref[at : at + 16, :].astype(F32)[:1]
        flags = jnp.concatenate([flags] * repeats, axis=1)[:, : blocks * slots]
        live = jnp.where(lane // slots == b, flags, live)
    box = dot(box_ref[...], chooser(depth, source_ref[...])).astype(BF16)
    box_wide_source = None
    del box_wide_source
    tokens = tokens_ref[...]
    wide = wide_ref[...]
    cut = 3 * part - fold
    for half, (early, late) in enumerate(((first_mine, mine_ref), (first_theirs, theirs_ref))):
        weights = late[...]
        kvq = dot(wide, weights).astype(BF16)
        q_low = dot(tokens, early[...][:, -cut:]).astype(BF16)
        query = jnp.concatenate([q_low, kvq[:, 2 * part :]], axis=1)
        box_kv = dot(box, weights[:, : 2 * part]).astype(BF16)
        attend_heads(
            query,
            [kvq[:, :part], box_kv[:, :part]],
            [kvq[:, part : 2 * part], box_kv[:, part : 2 * part]],
            [same, lambda s: jnp.where(live > 0, s, DEAD)],
            [same, same],
            acc_ref,
        )
        out_ref[:, half * part : (half + 1) * part] = (
            acc_ref[...] * jnp.tanh(gate_ref[half : half + 1, :])
        ).astype(BF16)


def cross_kernel(count_ref, tokens_ref, *refs, others):
    other_refs = refs[:others]
    mine_ref, theirs_ref, out_ref, acc_ref = refs[others:]
    part = out_ref.shape[1] // 2
    counts = [count_ref[0, j] for j in range(others)]
    score_edits = [same] + [
        lambda s, c=c: jnp.where(jnp.full((1, 1), c, F32) > 0, s, DEAD) for c in counts
    ]
    weight_edits = [same] + [lambda e, c=c: e * c for c in counts]
    for half, ref in enumerate((mine_ref, theirs_ref)):
        weights = ref[...]
        own = dot(tokens_ref[...], weights).astype(BF16)
        kv = [own[:, part:]] + [dot(o[...], weights[:, part:]).astype(BF16) for o in other_refs]
        attend_heads(
            own[:, :part],
            [x[:, :part] for x in kv],
            [x[:, part:] for x in kv],
            score_edits,
            weight_edits,
            acc_ref,
        )
        out_ref[:, half * part : (half + 1) * part] = acc_ref[...].astype(BF16)


def collect_kernel(half_ref, source_ref, cross_ref, time_ref, box_ref, out_ref):
    which = half_ref[0]
    total = None
    base = 0
    for ref in (cross_ref, time_ref, box_ref):
        part = ref.shape[1] // 2
        for half in range(2):
            side = which if half == 0 else 1 - which
            pick = chooser(part, source_ref[...], base + side * part)
            term = dot(ref[:, half * part : (half + 1) * part], pick)
            total = term if total is None else total + term
        base += 2 * part
    out_ref[...] = total.astype(BF16)


def final_kernel(half_ref, tokens_ref, attn_ref, mine_ref, theirs_ref, out_ref):
    width = mine_ref.shape[1]
    step = out_ref.shape[1] - width
    for half, ref in enumerate((mine_ref, theirs_ref)):
        side = half_ref[0] if half == 0 else 1 - half_ref[0]
        at = pl.ds(pl.multiple_of(side * step, 128), width)
        out_ref[:, at] = (tokens_ref[:, at].astype(F32) + dot(attn_ref[...], ref[...])).astype(
            BF16
        )


def call(kernel, outs, *args, scalars=0, scratch=(), name=None):
    vmem = pl.BlockSpec(memory_space=pltpu.VMEM)
    smem = pl.BlockSpec(memory_space=pltpu.SMEM)
    single = not isinstance(outs, list)
    result = pl.pallas_call(
        kernel,
        out_shape=outs if single else tuple(outs),
        in_specs=[smem] * scalars + [vmem] * (len(args) - scalars),
        out_specs=vmem if single else tuple(vmem for _ in outs),
        scratch_shapes=list(scratch),
        compiler_params=pltpu.CompilerParams(vmem_limit_bytes=VMEM_BYTES),
        name=name,
    )(*args)
    return result


def shaped(*dims):
    return jax.ShapeDtypeStruct(dims, BF16)


def per_device(frames_x, box_embed, box_count, frame_valid, cycle_link, w_qkv, w_out, box_gate):
    size = lax.axis_size("tm")
    cameras = lax.axis_size("view")
    depth = frames_x.shape[3]
    tokens = frames_x.reshape(-1, depth)
    count = tokens.shape[0]
    slots = box_embed.shape[2]
    boxes = box_embed.reshape(slots, depth)
    rows = w_qkv.shape[0]
    index = lax.axis_index("tm")
    half = lax.axis_index("view") % 2
    cw, tw, bw = (heads * HD // 2 for heads in (CROSS_HEADS, TIME_HEADS, BOX_HEADS))
    fold = depth // 3
    cut = 3 * bw - fold

    def pieces(side):
        def part(kind, base, width):
            at = kind * depth + base + side * width
            return w_qkv[:, at : at + width]

        cross = [part(kind, 0, cw) for kind in range(3)]
        timed = [part(kind, 2 * cw, tw) for kind in range(3)]
        q, k, v = [part(kind, 2 * cw + 2 * tw, bw) for kind in range(3)]
        out_width = -(-(depth // 2) // 128) * 128
        out_at = side * (depth - out_width)
        return (
            jnp.concatenate(timed + [q[:, :cut]], axis=1),
            jnp.concatenate([k, v, q[:, cut:]], axis=1),
            jnp.concatenate(cross, axis=1),
            w_out[:, out_at : out_at + out_width],
        )

    first, second, third, fourth = (
        jnp.where(half == 0, a, b) for a, b in zip(pieces(0), pieces(1))
    )
    live = (jnp.arange(slots, dtype=jnp.int32) < box_count[0, 0]) & (frame_valid[0, 0] == 1)
    flag_rows = jnp.broadcast_to(jnp.tile(live.astype(BF16), fold // slots)[None], (8, fold))
    box_rows = [boxes[:, j * fold : (j + 1) * fold] for j in range(3)]
    used = 3 * slots + 8 + rows
    block = -(-used // 16) * 16
    second = jnp.concatenate(
        box_rows + [flag_rows, second, jnp.zeros((block - used, fold), BF16)], axis=0
    )

    if cameras == 2:
        others = [swap(tokens, "view", 1)]
        link_counts = (cycle_link[:, :1] + cycle_link[:, 1:]).astype(F32)
    else:
        ring = range(cameras)
        others = [
            lax.ppermute(tokens, "view", [(i, (i + by) % cameras) for i in ring]) for by in (1, -1)
        ]
        link_counts = cycle_link.astype(F32)
    positions = count // size
    token_slices = lax.all_to_all(
        tokens.reshape(size, positions, depth), "tm", split_axis=0, concat_axis=0, tiled=True
    ).reshape(count, depth)

    gathered = []
    for number, piece in enumerate((first, second, third, fourth)):
        mine = gather_blocks(piece, *((1, 2) if number % 2 == 0 else (2, 1)))
        gathered.append((mine, swap(mine, "view", 1)))

    owners = index ^ jnp.array(block_order(size), jnp.int32)
    source = (owners[:, None] * rows + jnp.arange(rows)[None]).reshape(1, -1)
    wide_source = jnp.full((size, block), -1, jnp.int32)
    wide_source = wide_source.at[:, 3 * slots + 8 : used].set(source.reshape(size, rows))
    wide_source = wide_source.reshape(1, -1)

    ordered, wide, *ordered_others = call(
        functools.partial(order_kernel, others=len(others)),
        [shaped(count, depth), shaped(count, size * block)] + [shaped(count, depth) for _ in others],
        tokens, *others, source, wide_source,
        name="order",
    )
    timed = call(
        functools.partial(time_kernel, positions=positions),
        shaped(count, 2 * tw),
        token_slices, source, gathered[0][0][:, : 3 * tw], gathered[0][1][:, : 3 * tw],
        scratch=[pltpu.VMEM((count, tw), F32)],
        name="timed",
    )
    timed = lax.all_to_all(
        timed.reshape(size, positions, 2 * tw), "tm", split_axis=0, concat_axis=0, tiled=True
    ).reshape(count, 2 * tw)
    gates = box_gate.reshape(2, bw)
    gates = jnp.where(half == 0, gates, gates[::-1])
    boxed = call(
        functools.partial(box_kernel, slots=slots, blocks=size),
        shaped(count, 2 * bw),
        ordered, wide, wide_source, gates, *gathered[0], *gathered[1],
        scratch=[pltpu.VMEM((count, bw), F32), pltpu.VMEM((size * slots, depth), BF16)],
        name="boxed",
    )
    cross = call(
        functools.partial(cross_kernel, others=len(others)),
        shaped(count, 2 * cw),
        link_counts, ordered, *ordered_others, *gathered[2],
        scalars=1,
        scratch=[pltpu.VMEM((count, cw), F32)],
        name="cross",
    )
    which = half.reshape(1).astype(jnp.int32)
    attn = call(
        collect_kernel, shaped(count, depth), which, source, cross, timed, boxed,
        scalars=1, name="collect",
    )
    result = call(
        final_kernel, shaped(count, depth), which, tokens, attn, *gathered[3],
        scalars=1, name="final",
    )
    return result.reshape(frames_x.shape)


def solution(mesh):
    in_specs = (
        P("view", "tm", None, None),
        P("view", "tm", None, None),
        P("view", "tm"),
        P("view", "tm"),
        P("view", None),
        P("tm", None),
        P("tm", None),
        P(),
    )
    out_specs = P("view", "tm", None, None)
    return jax.shard_map(
        per_device, mesh=mesh, in_specs=in_specs, out_specs=out_specs, check_vma=False
    )
```

```python
import functools
import math

import jax
import jax.numpy as jnp
from jax import lax
from jax.experimental import pallas as pl
from jax.experimental.pallas import tpu as pltpu
from jax.sharding import PartitionSpec as P

HD = 72
CROSS_HEADS = 8
TIME_HEADS = 4
BOX_HEADS = 4
DEAD = -1e30
DEFINITE = 1e29
F32 = jnp.float32
BF16 = jnp.bfloat16
FLOPS_A_US = 1.1e9
BYTES_A_US = 3.6e6


def swap(value, axis, by):
    size = lax.axis_size(axis)
    return lax.ppermute(value, axis, [(i, i ^ by) for i in range(size)])


def tie(value, *before):
    return lax.optimization_barrier((value, *before))[0]


def tie_all(values, *before):
    return lax.optimization_barrier((*values, *before))[: len(values)]


def far_blocks(shard):
    size = lax.axis_size("tm")
    return jnp.concatenate([shard] + [swap(shard, "tm", d) for d in range(4, size, 4)], axis=0)


def near_step(value, step):
    size, cameras = lax.axis_size("tm"), lax.axis_size("view")
    pairs = [
        (v * size + i, v * size + (i ^ (1 << (v + step) % 2)))
        for v in range(cameras)
        for i in range(size)
    ]
    return lax.ppermute(value, ("view", "tm"), pairs)


def load_blocks(pieces, first, scratch, sems, columns):
    rows = pieces[0].shape[0]
    to = [0, (1 + first) * rows, (2 - first) * rows, 3 * rows]
    copies = [
        pltpu.make_async_copy(
            piece.at[:, columns], scratch.at[pl.ds(pl.multiple_of(at, 16), rows)], sems.at[j]
        )
        for j, (piece, at) in enumerate(zip(pieces, to))
    ]
    for copy in copies:
        copy.start()

    def wait():
        for copy in copies:
            copy.wait()

    return wait


def block_order(size):
    far = list(range(0, size, 4))
    return [f ^ low for low in range(4) for f in far]


def dot(a, b):
    return jnp.dot(a, b, preferred_element_type=F32)


def dot_t(a, b):
    return lax.dot_general(a, b, (((1,), (1,)), ((), ())), preferred_element_type=F32)


def chooser(rows, source, offset=0):
    row_ids = lax.broadcasted_iota(jnp.int32, (rows, source.shape[1]), 0)
    return (row_ids + offset == source).astype(F32).astype(BF16)


def attend_heads(query, keys, values, masks, offsets, store):
    width = query.shape[1]
    scale = HD ** (-0.5) * math.log2(math.e)
    for head in range(width // HD):
        low, high = head * HD, (head + 1) * HD
        left = low // 128 * 128
        right = min(width, -(-high // 128) * 128)
        lane = lax.broadcasted_iota(jnp.int32, (1, right - left), 1) + left
        mine = (lane >= low) & (lane < high)
        q = jnp.where(mine, query[:, left:right].astype(F32), 0.0).astype(BF16)
        scores = [dot_t(q, k[:, left:right]) for k in keys]
        scores = [s if m is None else jnp.where(m, s, DEAD) for s, m in zip(scores, masks)]
        tops = [jnp.max(s, axis=-1, keepdims=True) for s in scores]
        tops = [t if o is None else jnp.where(o < DEFINITE, t, DEAD) for t, o in zip(tops, offsets)]
        top = functools.reduce(jnp.maximum, tops)
        expos = [
            jnp.exp2((s - (top if o is None else top + o)) * scale) for s, o in zip(scores, offsets)
        ]
        total = sum(jnp.sum(e, axis=-1, keepdims=True) for e in expos)
        out = sum(dot(e.astype(BF16), v[:, left:right]) for e, v in zip(expos, values))
        store(left, right, mine, out / total)


def keep_rows(half, ref, at, end, left, right, mine, result):
    ref[half, at:end, left:right] = jnp.where(mine, result, ref[half, at:end, left:right])


def keep_in(ref):
    def store(left, right, mine, result):
        ref[:, left:right] = jnp.where(mine, result, ref[:, left:right])

    return store


def send_kernel(
    half_ref, count_ref, valid_ref, qkv_ref, w_out_ref, box_ref, early_ref, cross_ref, closing_ref,
    *, parts,
):
    cw, tw, bw = parts
    block, width = early_ref.shape
    rows, depth = w_out_ref.shape
    lane = lax.broadcasted_iota(jnp.int32, (8, 128), 1)
    live = (lane < count_ref[0, 0]) & (lane < box_ref.shape[0])
    flags = jnp.where(live & (jnp.full((8, 128), valid_ref[0, 0]) == 1), 1.0, 0.0)
    boxes = box_ref[...].astype(F32)
    carried = [boxes[:8], boxes[8:], flags]
    filled = 2 * depth + 128
    carried = jnp.concatenate(carried + [jnp.zeros((8, 3 * width - filled), F32)], axis=1)
    carried = [carried[:, j * width : (j + 1) * width] for j in range(3)]

    def side_columns(side):
        def part(base, size):
            at = [kind * depth + base + side * size for kind in range(3)]
            return [qkv_ref[:, a : a + size].astype(F32) for a in at]

        def fill(x, to, axis):
            size = list(x.shape)
            size[axis] = to - size[axis]
            return jnp.concatenate([x, jnp.zeros(size, F32)], axis) if size[axis] else x

        weights = jnp.concatenate(part(2 * cw, tw) + part(2 * cw + 2 * tw, bw), axis=1)
        early = jnp.concatenate(carried + [fill(weights, width, 1)], axis=0)
        early_ref[...] = fill(early, block, 0).astype(BF16)
        cross = jnp.concatenate(part(0, cw), axis=1)
        cross_ref[...] = fill(cross, cross_ref.shape[1], 1).astype(BF16)
        at = side * (depth - closing_ref.shape[1])
        closing_ref[...] = w_out_ref[:, at : at + closing_ref.shape[1]]

    for side in range(2):
        pl.when(half_ref[0] == side)(functools.partial(side_columns, side))


def order_kernel(tokens_ref, *refs, others):
    other_refs = refs[:others]
    source_ref, wide_source_ref, out_ref, wide_ref, pick_ref = refs[others : others + 5]
    out_refs = refs[others + 5 :]
    depth = tokens_ref.shape[1]
    pick = chooser(depth, source_ref[...])
    out_ref[...] = dot(tokens_ref[...], pick).astype(BF16)
    for a, b in zip(other_refs, out_refs):
        b[...] = dot(a[...], pick).astype(BF16)
    pick_ref[...] = chooser(depth, wide_source_ref[...])
    wide_ref[...] = dot(tokens_ref[...], pick_ref[...]).astype(BF16)


def regroup(rows, positions):
    frames = rows // positions
    to = lax.broadcasted_iota(jnp.int32, (rows, 1), 0)
    source = (to % frames) * positions + to // frames
    return (lax.broadcasted_iota(jnp.int32, (1, rows), 1) == source).astype(F32).astype(BF16)


def widen_kernel(tokens_ref, pick_ref, wide_ref, *, positions):
    tokens = tokens_ref[...]
    tokens = dot(regroup(tokens.shape[0], positions), tokens).astype(BF16)
    wide_ref[...] = dot(tokens, pick_ref[...]).astype(BF16)


def load_halves(half_ref, piece_refs, scratch, sems, columns):
    return [
        load_blocks(
            piece_refs[4 * j : 4 * j + 4],
            half_ref[0] if j == 0 else 1 - half_ref[0],
            scratch.at[j],
            sems.at[j],
            columns,
        )
        for j in range(2)
    ]


def time_kernel(half_ref, wide_ref, *refs, positions):
    piece_refs, (out_ref, acc_ref, weight_ref, sems) = refs[:8], refs[8:]
    waits = load_halves(half_ref, piece_refs, weight_ref, sems, pl.ds(0, weight_ref.shape[2]))
    rows = wide_ref.shape[0]
    frames = rows // positions
    part = out_ref.shape[1] // 2
    step = max(frames, 128) if rows % max(frames, 128) == 0 else rows
    group = lax.broadcasted_iota(jnp.int32, (step, 1), 0) // frames
    group_t = lax.broadcasted_iota(jnp.int32, (1, step), 1) // frames
    live = group == group_t
    wide = wide_ref[...]
    for half in range(2):
        waits[half]()
        qkv = dot(wide, weight_ref[half]).astype(BF16)
        q, k, v = (qkv[:, j * part : (j + 1) * part] for j in range(3))
        for at in range(0, rows, step):
            end = at + step
            attend_heads(
                q[at:end], [k[at:end]], [v[at:end]], [live], [None],
                functools.partial(keep_rows, half, acc_ref, at, end),
            )
    timed = jnp.concatenate([acc_ref[0].astype(BF16), acc_ref[1].astype(BF16)], axis=1)
    back = lax.dot_general(
        regroup(rows, positions), timed, (((0,), (0,)), ((), ())), preferred_element_type=F32
    )
    out_ref[...] = back.astype(BF16)


def box_kernel(
    half_ref, wide_ref, pick_ref, gate_ref, *refs, slots, blocks, skip
):
    piece_refs = refs[:8]
    out_ref, acc_ref, box_ref, flag_ref, weight_ref, carried_ref, sems, carried_sems = refs[8:]
    part = out_ref.shape[1] // 2
    depth = box_ref.shape[1]
    block, width = carried_ref.shape[0] // blocks, carried_ref.shape[1]
    left = skip // 128 * 128
    carried = load_blocks(
        piece_refs[:4], half_ref[0], carried_ref, carried_sems, pl.ds(0, width)
    )
    waits = load_halves(
        half_ref, piece_refs, weight_ref, sems, pl.ds(left, weight_ref.shape[2])
    )
    wide = wide_ref[...]
    shift = skip - left
    carried()
    for b in range(blocks):
        at = b * block
        top = carried_ref[at : at + 16, :].astype(F32)
        low = carried_ref[at + 16 : at + 32, :].astype(F32)[:8]
        spread = 2 * width - depth
        rest = depth - spread
        to = b * 8
        box_ref[to : to + 8, :width] = top[:8]
        box_ref[to : to + 8, width:] = top[8:, : depth - width]
        to += blocks * 8
        box_ref[to : to + 8, :spread] = top[8:, depth - width :]
        box_ref[to : to + 8, spread:] = low[:, :rest]
        flag_ref[b : b + 1, :] = low[:1, rest : rest + 128]
    slot_lane = lax.broadcasted_iota(jnp.int32, (1, blocks * slots), 1)
    group = slot_lane // (8 * blocks)
    slot = group * 8 + slot_lane % 8
    of_block = (slot_lane // 8) % blocks
    spread_slots = (
        lax.broadcasted_iota(jnp.int32, (128, blocks * slots), 0) == slot
    ).astype(F32)
    flags = dot(flag_ref[...].astype(BF16), spread_slots.astype(BF16))
    mine = lax.broadcasted_iota(jnp.int32, (blocks, blocks * slots), 0) == of_block
    live = jnp.sum(jnp.where(mine, flags, 0.0), axis=0, keepdims=True)
    box = dot(box_ref[...].astype(BF16), pick_ref[...]).astype(BF16)
    for half in range(2):
        waits[half]()
        weights = weight_ref[half]
        qkv = dot(wide, weights).astype(BF16)[:, shift : shift + 3 * part]
        box_kv = dot(box, weights).astype(BF16)[:, shift + part : shift + 3 * part]
        attend_heads(
            qkv[:, :part],
            [qkv[:, part : 2 * part], box_kv[:, :part]],
            [qkv[:, 2 * part :], box_kv[:, part:]],
            [None, live > 0],
            [None, None],
            keep_in(acc_ref),
        )
        out_ref[:, half * part : (half + 1) * part] = (
            acc_ref[...] * jnp.tanh(gate_ref[half : half + 1, :])
        ).astype(BF16)


def cross_kernel(half_ref, count_ref, tokens_ref, *refs, others):
    other_refs, piece_refs = refs[:others], refs[others : others + 8]
    out_ref, acc_ref, weight_ref, sems = refs[others + 8 :]
    waits = load_halves(half_ref, piece_refs, weight_ref, sems, pl.ds(0, weight_ref.shape[2]))
    part = out_ref.shape[1] // 2
    unit = math.log(2) / HD ** (-0.5)
    offsets = [None]
    for j in range(others):
        count = jnp.full((1, 1), count_ref[0, j], F32)
        offsets.append(jnp.where(count > 1.5, -unit, jnp.where(count > 0.5, 0.0, -DEAD)))
    for half in range(2):
        waits[half]()
        weights = weight_ref[half]
        own = dot(tokens_ref[...], weights).astype(BF16)
        at = part // 128 * 128
        kv = [own[:, part : 3 * part]] + [
            dot(o[...], weights[:, at:]).astype(BF16)[:, part - at : 3 * part - at]
            for o in other_refs
        ]
        attend_heads(
            own[:, :part],
            [x[:, :part] for x in kv],
            [x[:, part:] for x in kv],
            [None] * (1 + others),
            offsets,
            keep_in(acc_ref),
        )
        out_ref[:, half * part : (half + 1) * part] = acc_ref[...].astype(BF16)


def collect_kernel(half_ref, source_ref, cross_ref, time_ref, box_ref, out_ref):
    which = half_ref[0]
    total = None
    base = 0
    for ref in (cross_ref, time_ref, box_ref):
        part = ref.shape[1] // 2
        for half in range(2):
            side = which if half == 0 else 1 - which
            pick = chooser(part, source_ref[...], base + side * part)
            term = dot(ref[:, half * part : (half + 1) * part], pick)
            total = term if total is None else total + term
        base += 2 * part
    out_ref[...] = total.astype(BF16)


def final_kernel(half_ref, tokens_ref, attn_ref, *refs):
    piece_refs, (out_ref, weight_ref, sems) = refs[:8], refs[8:]
    width = weight_ref.shape[2]
    waits = load_halves(half_ref, piece_refs, weight_ref, sems, pl.ds(0, width))
    step = out_ref.shape[1] - width
    for half in range(2):
        waits[half]()
        side = half_ref[0] if half == 0 else 1 - half_ref[0]
        at = pl.ds(pl.multiple_of(side * step, 128), width)
        out_ref[:, at] = (tokens_ref[:, at].astype(F32) + dot(attn_ref[...], weight_ref[half])).astype(
            BF16
        )


def call(kernel, outs, *args, scalars=0, scratch=(), pieces=(), name=None, vmem_mib=24, us=4):
    vmem = pl.BlockSpec(memory_space=pltpu.VMEM)
    smem = pl.BlockSpec(memory_space=pltpu.SMEM)
    anywhere = pl.BlockSpec(memory_space=pl.ANY)
    single = not isinstance(outs, list)
    return pl.pallas_call(
        kernel,
        out_shape=outs if single else tuple(outs),
        in_specs=[smem] * scalars + [vmem] * (len(args) - scalars) + [anywhere] * len(pieces),
        out_specs=vmem if single else tuple(vmem for _ in outs),
        scratch_shapes=list(scratch),
        compiler_params=pltpu.CompilerParams(vmem_limit_bytes=vmem_mib * 2**20),
        cost_estimate=pl.CostEstimate(
            flops=int(us * FLOPS_A_US), bytes_accessed=int(us * BYTES_A_US), transcendentals=0
        ),
        name=name,
    )(*args, *pieces)


def whole_tiles(width):
    return -(-width // 128) * 128


def shaped(*dims):
    return jax.ShapeDtypeStruct(dims, BF16)


def per_device(frames_x, box_embed, box_count, frame_valid, cycle_link, w_qkv, w_out, box_gate):
    size = lax.axis_size("tm")
    cameras = lax.axis_size("view")
    depth = frames_x.shape[3]
    tokens = frames_x.reshape(-1, depth)
    count = tokens.shape[0]
    slots = box_embed.shape[2]
    boxes = box_embed.reshape(slots, depth)
    rows = w_qkv.shape[0]
    index = lax.axis_index("tm")
    half = lax.axis_index("view") % 2
    cw, tw, bw = (heads * HD // 2 for heads in (CROSS_HEADS, TIME_HEADS, BOX_HEADS))

    width, out_width = whole_tiles(3 * (tw + bw)), whole_tiles(depth // 2)
    cross_width = whole_tiles(3 * cw)
    used = 24 + rows
    block = -(-used // 16) * 16
    which = half.reshape(1).astype(jnp.int32)
    early, crossing, closing = call(
        functools.partial(send_kernel, parts=(cw, tw, bw)),
        [shaped(block, width), shaped(rows, cross_width), shaped(rows, out_width)],
        which, box_count, frame_valid, w_qkv, w_out, boxes,
        scalars=3, name="send", us=2,
    )

    if cameras == 2:
        others = [swap(tokens, "view", 1)]
        link_counts = (cycle_link[:, :1] + cycle_link[:, 1:]).astype(F32)
    else:
        ring = range(cameras)
        others = [
            lax.ppermute(tokens, "view", [(i, (i + by) % cameras) for i in ring]) for by in (1, -1)
        ]
        link_counts = cycle_link.astype(F32)
    owners = index ^ jnp.array(block_order(size), jnp.int32)
    source = (owners[:, None] * rows + jnp.arange(rows)[None]).reshape(1, -1)
    wide_source = jnp.full((size, block), -1, jnp.int32)
    wide_source = wide_source.at[:, 24:used].set(source.reshape(size, rows)).reshape(1, -1)

    ordered, wide, pick, *ordered_others = call(
        functools.partial(order_kernel, others=len(others)),
        [shaped(count, depth), shaped(count, size * block), shaped(depth, size * block)]
        + [shaped(count, depth) for _ in others],
        tokens, *others, source, wide_source,
        name="order", us=6,
    )

    def near_blocks(far, *before):
        one = near_step(far, 0)
        two = near_step(far, 1)
        return far, one, two, near_step(tie(one, *before) if before else one, 1)

    def with_other_core(blocks):
        return (*blocks, *(swap(b, "view", 1) for b in blocks))

    def weight_scratch(far_rows, columns):
        return [pltpu.VMEM((2, 4 * far_rows, columns), BF16), pltpu.SemaphoreType.DMA((2, 4))]

    early = far_blocks(early)
    crossing = far_blocks(tie(crossing, early))
    positions = count // size
    token_slices = lax.all_to_all(
        tie(tokens, early).reshape(size, positions, depth),
        "tm", split_axis=0, concat_axis=0, tiled=True,
    ).reshape(count, depth)
    early = near_blocks(early, ordered)
    wide_slices = call(
        functools.partial(widen_kernel, positions=positions),
        shaped(count, size * block), token_slices, pick, name="widen", us=2,
    )
    closing = far_blocks(tie(closing, token_slices))
    early_rows = early[0].shape[0]
    early_near = early
    early = with_other_core(early)
    timed = call(
        functools.partial(time_kernel, positions=positions),
        shaped(count, 2 * tw),
        which, wide_slices,
        scalars=1,
        pieces=early,
        scratch=[pltpu.VMEM((2, count, tw), F32)]
        + weight_scratch(early_rows, whole_tiles(3 * tw)),
        name="timed", us=5,
    )
    timed_here = timed
    crossing = near_blocks(tie(crossing, early_near[1], early_near[2]), timed_here)
    timed = lax.all_to_all(
        timed.reshape(size, positions, 2 * tw), "tm", split_axis=0, concat_axis=0, tiled=True
    ).reshape(count, 2 * tw)
    closing = near_blocks(closing, timed_here)
    link_counts = tie(link_counts, timed_here)
    gates = box_gate.reshape(2, bw)
    gates = jnp.where(half == 0, gates, gates[::-1])
    boxed = call(
        functools.partial(box_kernel, slots=slots, blocks=size, skip=3 * tw),
        shaped(count, 2 * bw),
        which, wide, pick, gates,
        scalars=1,
        pieces=early,
        scratch=[
            pltpu.VMEM((count, bw), F32),
            pltpu.VMEM((size * slots, depth), F32),
            pltpu.VMEM((size, 128), F32),
            *weight_scratch(early_rows, width - 3 * tw // 128 * 128)[:1],
            pltpu.VMEM((size * block, width), BF16),
            *weight_scratch(early_rows, width)[1:],
            pltpu.SemaphoreType.DMA((4,)),
        ],
        name="boxed", us=7,
    )
    cross_rows = crossing[0].shape[0]
    cross = call(
        functools.partial(cross_kernel, others=len(others)),
        shaped(count, 2 * cw),
        which, link_counts, ordered, *ordered_others,
        scalars=2,
        pieces=with_other_core(crossing),
        scratch=[pltpu.VMEM((count, cw), F32)] + weight_scratch(cross_rows, cross_width),
        name="cross", us=9,
    )
    attn = call(
        collect_kernel, shaped(count, depth), which, source, cross, timed, boxed,
        scalars=1, name="collect", us=2,
    )
    result = call(
        final_kernel, shaped(count, depth), which, tokens, attn,
        scalars=1,
        pieces=with_other_core(closing),
        scratch=weight_scratch(closing[0].shape[0], out_width),
        name="final", us=4,
    )
    return result.reshape(frames_x.shape)


def solution(mesh):
    in_specs = (
        P("view", "tm", None, None),
        P("view", "tm", None, None),
        P("view", "tm"),
        P("view", "tm"),
        P("view", None),
        P("tm", None),
        P("tm", None),
        P(),
    )
    out_specs = P("view", "tm", None, None)
    return jax.shard_map(
        per_device, mesh=mesh, in_specs=in_specs, out_specs=out_specs, check_vma=False
    )
```

```python
import functools
import math

import jax
import jax.numpy as jnp
from jax import lax
from jax.experimental import pallas as pl
from jax.experimental.pallas import tpu as pltpu
from jax.sharding import PartitionSpec as P

HD = 72
CROSS_HEADS = 8
TIME_HEADS = 4
BOX_HEADS = 4
DEAD = -1e30
DEFINITE = 1e29
F32 = jnp.float32
BF16 = jnp.bfloat16
FLOPS_A_US = 1.1e9
BYTES_A_US = 3.6e6


def swap(value, axis, by):
    size = lax.axis_size(axis)
    return lax.ppermute(value, axis, [(i, i ^ by) for i in range(size)])


def tie(value, *before):
    return lax.optimization_barrier((value, *before))[0]


def far_blocks(shard):
    size = lax.axis_size("tm")
    parts = [swap(shard, "tm", d) for d in range(4, size, 4)]
    return jnp.concatenate([shard] + parts, axis=0)


def near_step(value, step):
    size, cameras = lax.axis_size("tm"), lax.axis_size("view")
    pairs = [
        (v * size + i, v * size + (i ^ (1 << (v + step) % 2)))
        for v in range(cameras)
        for i in range(size)
    ]
    return lax.ppermute(value, ("view", "tm"), pairs)


def load_blocks(pieces, first, scratch, sems, columns):
    rows = pieces[0].shape[0]
    to = [0, (1 + first) * rows, (2 - first) * rows, 3 * rows]
    copies = [
        pltpu.make_async_copy(
            piece.at[:, columns], scratch.at[pl.ds(pl.multiple_of(at, 16), rows)], sems.at[j]
        )
        for j, (piece, at) in enumerate(zip(pieces, to))
    ]
    for copy in copies:
        copy.start()

    def wait():
        for copy in copies:
            copy.wait()

    return wait


def block_order(size):
    far = list(range(0, size, 4))
    return [f ^ low for low in range(4) for f in far]


def dot(a, b):
    return jnp.dot(a, b, preferred_element_type=F32)


def dot_t(a, b):
    return lax.dot_general(a, b, (((1,), (1,)), ((), ())), preferred_element_type=F32)


def chooser(rows, source, offset=0):
    row_ids = lax.broadcasted_iota(jnp.int32, (rows, source.shape[1]), 0)
    return (row_ids + offset == source).astype(F32).astype(BF16)


def attend_heads(query, keys, values, masks, offsets, store):
    width = query.shape[1]
    scale = HD ** (-0.5) * math.log2(math.e)
    for head in range(width // HD):
        low, high = head * HD, (head + 1) * HD
        left = low // 128 * 128
        right = min(width, -(-high // 128) * 128)
        spare = right - 1 - left if high < right else 0
        lane = lax.broadcasted_iota(jnp.int32, (1, right - left), 1) + left
        mine = (lane >= low) & (lane < high)
        counts = lane == spare + left
        q = jnp.where(mine, query[:, left:right].astype(F32), 0.0).astype(BF16)
        scores = dot_t(q, jnp.concatenate([k[:, left:right] for k in keys], axis=0))
        ends = [0]
        for k in keys:
            ends.append(ends[-1] + k.shape[0])
        scores = [scores[:, a:b] for a, b in zip(ends[:-1], ends[1:])]
        scores = [s if m is None else jnp.where(m, s, DEAD) for s, m in zip(scores, masks)]
        tops = [
            functools.reduce(
                jnp.maximum, [s[:, at : at + 128] for at in range(0, s.shape[1], 128)]
            )
            for s in scores
        ]
        tops = [t if o is None else jnp.where(o < DEFINITE, t, DEAD) for t, o in zip(tops, offsets)]
        top = jnp.max(functools.reduce(jnp.maximum, tops), axis=-1, keepdims=True)
        expos = [
            jnp.exp2((s - (top if o is None else top + o)) * scale).astype(BF16)
            for s, o in zip(scores, offsets)
        ]
        value = jnp.concatenate([v[:, left:right] for v in values], axis=0)
        value = jnp.where(counts, 1.0, value.astype(F32)).astype(BF16)
        out = dot(jnp.concatenate(expos, axis=1), value)
        store(left, right, mine, out / out[:, spare : spare + 1])


def keep_rows(half, ref, at, end, left, right, mine, result):
    ref[half, at:end, left:right] = jnp.where(mine, result, ref[half, at:end, left:right])


def keep_in(ref):
    def store(left, right, mine, result):
        ref[:, left:right] = jnp.where(mine, result, ref[:, left:right])

    return store


def send_kernel(
    half_ref, count_ref, valid_ref, qkv_hbm, w_out_hbm, box_hbm, early_ref, cross_ref, closing_ref,
    qkv_ref, w_out_ref, box_ref, sems, *, parts,
):
    copies = [
        pltpu.make_async_copy(a, b, sems.at[j])
        for j, (a, b) in enumerate(
            ((qkv_hbm, qkv_ref), (box_hbm, box_ref), (w_out_hbm, w_out_ref))
        )
    ]
    for copy in copies:
        copy.start()
    for copy in copies:
        copy.wait()
    cw, tw, bw = parts
    block, width = early_ref.shape
    rows, depth = w_out_ref.shape
    lane = lax.broadcasted_iota(jnp.int32, (8, 128), 1)
    live = (lane < count_ref[0, 0]) & (lane < box_ref.shape[0])
    flags = jnp.where(live & (jnp.full((8, 128), valid_ref[0, 0]) == 1), 1.0, 0.0)
    boxes = box_ref[...].astype(F32)
    carried = [boxes[:8], boxes[8:], flags]
    filled = 2 * depth + 128
    carried = jnp.concatenate(carried + [jnp.zeros((8, 3 * width - filled), F32)], axis=1)
    carried = [carried[:, j * width : (j + 1) * width] for j in range(3)]

    def side_columns(side):
        def part(base, size):
            at = [kind * depth + base + side * size for kind in range(3)]
            return [qkv_ref[:, a : a + size].astype(F32) for a in at]

        def fill(x, to, axis):
            size = list(x.shape)
            size[axis] = to - size[axis]
            return jnp.concatenate([x, jnp.zeros(size, F32)], axis) if size[axis] else x

        weights = jnp.concatenate(part(2 * cw, tw) + part(2 * cw + 2 * tw, bw), axis=1)
        early = jnp.concatenate(carried + [fill(weights, width, 1)], axis=0)
        early_ref[...] = fill(early, block, 0).astype(BF16)
        cross = jnp.concatenate(part(0, cw), axis=1)
        cross_ref[...] = fill(cross, cross_ref.shape[1], 1).astype(BF16)
        at = side * (depth - closing_ref.shape[1])
        closing_ref[...] = w_out_ref[:, at : at + closing_ref.shape[1]]

    for side in range(2):
        pl.when(half_ref[0] == side)(functools.partial(side_columns, side))


def order_kernel(tokens_ref, *refs, others):
    other_refs = refs[:others]
    source_ref, wide_source_ref, out_ref, wide_ref = refs[others : others + 4]
    out_refs = refs[others + 4 :]
    depth = tokens_ref.shape[1]
    pick = chooser(depth, source_ref[...])
    out_ref[...] = dot(tokens_ref[...], pick).astype(BF16)
    for a, b in zip(other_refs, out_refs):
        b[...] = dot(a[...], pick).astype(BF16)
    wide_ref[...] = dot(tokens_ref[...], chooser(depth, wide_source_ref[...])).astype(BF16)


def regroup(rows, positions):
    frames = rows // positions
    to = lax.broadcasted_iota(jnp.int32, (rows, 1), 0)
    source = (to % frames) * positions + to // frames
    return (lax.broadcasted_iota(jnp.int32, (1, rows), 1) == source).astype(F32).astype(BF16)


def widen_kernel(tokens_ref, source_ref, wide_ref, *, positions):
    tokens = tokens_ref[...]
    tokens = dot(regroup(tokens.shape[0], positions), tokens).astype(BF16)
    wide_ref[...] = dot(tokens, chooser(tokens.shape[1], source_ref[...])).astype(BF16)


def load_halves(half_ref, piece_refs, scratch, sems, columns):
    return [
        load_blocks(
            piece_refs[4 * j : 4 * j + 4],
            half_ref[0] if j == 0 else 1 - half_ref[0],
            scratch.at[j],
            sems.at[j],
            columns,
        )
        for j in range(2)
    ]


def time_kernel(half_ref, wide_ref, *refs, positions):
    piece_refs, (out_ref, acc_ref, weight_ref, sems) = refs[:8], refs[8:]
    waits = load_halves(half_ref, piece_refs, weight_ref, sems, pl.ds(0, weight_ref.shape[2]))
    rows = wide_ref.shape[0]
    frames = rows // positions
    part = out_ref.shape[1] // 2
    step = max(frames, 128) if rows % max(frames, 128) == 0 else rows
    group = lax.broadcasted_iota(jnp.int32, (step, 1), 0) // frames
    group_t = lax.broadcasted_iota(jnp.int32, (1, step), 1) // frames
    live = group == group_t
    wide = wide_ref[...]
    for half in range(2):
        waits[half]()
        qkv = dot(wide, weight_ref[half]).astype(BF16)
        q, k, v = (qkv[:, j * part : (j + 1) * part] for j in range(3))
        for at in range(0, rows, step):
            end = at + step
            attend_heads(
                q[at:end], [k[at:end]], [v[at:end]], [live], [None],
                functools.partial(keep_rows, half, acc_ref, at, end),
            )
    timed = jnp.concatenate([acc_ref[0].astype(BF16), acc_ref[1].astype(BF16)], axis=1)
    back = lax.dot_general(
        regroup(rows, positions), timed, (((0,), (0,)), ((), ())), preferred_element_type=F32
    )
    out_ref[...] = back.astype(BF16)


def box_kernel(
    half_ref, wide_ref, source_ref, gate_ref, *refs, slots, blocks, skip
):
    piece_refs = refs[:8]
    out_ref, acc_ref, box_ref, flag_ref, weight_ref, carried_ref, sems, carried_sems = refs[8:]
    part = out_ref.shape[1] // 2
    depth = box_ref.shape[1]
    block, width = carried_ref.shape[0] // blocks, carried_ref.shape[1]
    left = skip // 128 * 128
    carried = load_blocks(
        piece_refs[:4], half_ref[0], carried_ref, carried_sems, pl.ds(0, width)
    )
    waits = load_halves(
        half_ref, piece_refs, weight_ref, sems, pl.ds(left, weight_ref.shape[2])
    )
    wide = wide_ref[...]
    shift = skip - left
    carried()
    for b in range(blocks):
        at = b * block
        top = carried_ref[at : at + 16, :].astype(F32)
        low = carried_ref[at + 16 : at + 32, :].astype(F32)[:8]
        spread = 2 * width - depth
        rest = depth - spread
        to = b * 8
        box_ref[to : to + 8, :width] = top[:8]
        box_ref[to : to + 8, width:] = top[8:, : depth - width]
        to += blocks * 8
        box_ref[to : to + 8, :spread] = top[8:, depth - width :]
        box_ref[to : to + 8, spread:] = low[:, :rest]
        flag_ref[b : b + 1, :] = low[:1, rest : rest + 128]
    slot_lane = lax.broadcasted_iota(jnp.int32, (1, blocks * slots), 1)
    group = slot_lane // (8 * blocks)
    slot = group * 8 + slot_lane % 8
    of_block = (slot_lane // 8) % blocks
    spread_slots = (
        lax.broadcasted_iota(jnp.int32, (128, blocks * slots), 0) == slot
    ).astype(F32)
    flags = dot(flag_ref[...].astype(BF16), spread_slots.astype(BF16))
    mine = lax.broadcasted_iota(jnp.int32, (blocks, blocks * slots), 0) == of_block
    live = jnp.sum(jnp.where(mine, flags, 0.0), axis=0, keepdims=True)
    box = dot(box_ref[...].astype(BF16), chooser(depth, source_ref[...])).astype(BF16)
    for half in range(2):
        waits[half]()
        weights = weight_ref[half]
        qkv = dot(wide, weights).astype(BF16)[:, shift : shift + 3 * part]
        box_kv = dot(box, weights).astype(BF16)[:, shift + part : shift + 3 * part]
        attend_heads(
            qkv[:, :part],
            [qkv[:, part : 2 * part], box_kv[:, :part]],
            [qkv[:, 2 * part :], box_kv[:, part:]],
            [None, live > 0],
            [None, None],
            keep_in(acc_ref),
        )
        out_ref[:, half * part : (half + 1) * part] = (
            acc_ref[...] * jnp.tanh(gate_ref[half : half + 1, :])
        ).astype(BF16)


def cross_kernel(half_ref, count_ref, tokens_ref, *refs, others):
    other_refs, piece_refs = refs[:others], refs[others : others + 8]
    out_ref, acc_ref, weight_ref, sems = refs[others + 8 :]
    waits = load_halves(half_ref, piece_refs, weight_ref, sems, pl.ds(0, weight_ref.shape[2]))
    part = out_ref.shape[1] // 2
    unit = math.log(2) / HD ** (-0.5)
    offsets = [None]
    for j in range(others):
        count = jnp.full((1, 1), count_ref[0, j], F32)
        offsets.append(jnp.where(count > 1.5, -unit, jnp.where(count > 0.5, 0.0, -DEAD)))
    for half in range(2):
        waits[half]()
        weights = weight_ref[half]
        own = dot(tokens_ref[...], weights).astype(BF16)
        at = part // 128 * 128
        kv = [own[:, part : 3 * part]] + [
            dot(o[...], weights[:, at:]).astype(BF16)[:, part - at : 3 * part - at]
            for o in other_refs
        ]
        attend_heads(
            own[:, :part],
            [x[:, :part] for x in kv],
            [x[:, part:] for x in kv],
            [None] * (1 + others),
            offsets,
            keep_in(acc_ref),
        )
        out_ref[:, half * part : (half + 1) * part] = acc_ref[...].astype(BF16)


def final_kernel(half_ref, tokens_ref, source_ref, cross_ref, time_ref, box_ref, *refs):
    piece_refs, (out_ref, weight_ref, sems) = refs[:8], refs[8:]
    width = weight_ref.shape[2]
    waits = load_halves(half_ref, piece_refs, weight_ref, sems, pl.ds(0, width))
    which = half_ref[0]
    attn = None
    base = 0
    for ref in (cross_ref, time_ref, box_ref):
        part = ref.shape[1] // 2
        for half in range(2):
            side = which if half == 0 else 1 - which
            pick = chooser(part, source_ref[...], base + side * part)
            term = dot(ref[:, half * part : (half + 1) * part], pick)
            attn = term if attn is None else attn + term
        base += 2 * part
    attn = attn.astype(BF16)
    step = out_ref.shape[1] - width
    for half in range(2):
        waits[half]()
        side = which if half == 0 else 1 - which
        at = pl.ds(pl.multiple_of(side * step, 128), width)
        out_ref[:, at] = (tokens_ref[:, at].astype(F32) + dot(attn, weight_ref[half])).astype(BF16)


def call(
    kernel, outs, *args, scalars=0, scratch=(), pieces=(), name=None, vmem_mib=24, us=4
):
    vmem = pl.BlockSpec(memory_space=pltpu.VMEM)
    smem = pl.BlockSpec(memory_space=pltpu.SMEM)
    hbm = pl.BlockSpec(memory_space=pltpu.HBM)
    single = not isinstance(outs, list)
    return pl.pallas_call(
        kernel,
        out_shape=outs if single else tuple(outs),
        in_specs=[smem] * scalars + [vmem] * (len(args) - scalars) + [hbm] * len(pieces),
        out_specs=vmem if single else tuple(vmem for _ in outs),
        scratch_shapes=list(scratch),
        compiler_params=pltpu.CompilerParams(vmem_limit_bytes=vmem_mib * 2**20),
        cost_estimate=pl.CostEstimate(
            flops=int(us * FLOPS_A_US), bytes_accessed=int(us * BYTES_A_US), transcendentals=0
        ),
        name=name,
    )(*args, *pieces)


def whole_tiles(width):
    return -(-width // 128) * 128


def shaped(*dims):
    return jax.ShapeDtypeStruct(dims, BF16)


def per_device(frames_x, box_embed, box_count, frame_valid, cycle_link, w_qkv, w_out, box_gate):
    size = lax.axis_size("tm")
    cameras = lax.axis_size("view")
    depth = frames_x.shape[3]
    tokens = frames_x.reshape(-1, depth)
    count = tokens.shape[0]
    slots = box_embed.shape[2]
    boxes = box_embed.reshape(slots, depth)
    rows = w_qkv.shape[0]
    index = lax.axis_index("tm")
    half = lax.axis_index("view") % 2
    cw, tw, bw = (heads * HD // 2 for heads in (CROSS_HEADS, TIME_HEADS, BOX_HEADS))

    width, out_width = whole_tiles(3 * (tw + bw)), whole_tiles(depth // 2)
    cross_width = whole_tiles(3 * cw)
    used = 24 + rows
    block = -(-used // 16) * 16
    which = half.reshape(1).astype(jnp.int32)
    early, crossing, closing = call(
        functools.partial(send_kernel, parts=(cw, tw, bw)),
        [shaped(block, width), shaped(rows, cross_width), shaped(rows, out_width)],
        which, box_count, frame_valid,
        scalars=3,
        pieces=(w_qkv, w_out, boxes),
        scratch=[pltpu.VMEM(x.shape, BF16) for x in (w_qkv, w_out, boxes)]
        + [pltpu.SemaphoreType.DMA((3,))],
        name="send", us=2,
    )

    if cameras == 2:
        others = [swap(tokens, "view", 1)]
        link_counts = (cycle_link[:, :1] + cycle_link[:, 1:]).astype(F32)
    else:
        ring = range(cameras)
        others = [
            lax.ppermute(tokens, "view", [(i, (i + by) % cameras) for i in ring]) for by in (1, -1)
        ]
        link_counts = cycle_link.astype(F32)
    owners = index ^ jnp.array(block_order(size), jnp.int32)
    source = (owners[:, None] * rows + jnp.arange(rows)[None]).reshape(1, -1)
    wide_source = jnp.full((size, block), -1, jnp.int32)
    wide_source = wide_source.at[:, 24:used].set(source.reshape(size, rows)).reshape(1, -1)

    def near_blocks(far, *before):
        one = near_step(far, 0)
        two = near_step(far, 1)
        return far, one, two, near_step(tie(one, *before), 1)

    def with_other_core(blocks):
        return (*blocks, *(swap(b, "view", 1) for b in blocks))

    def weight_scratch(far_rows, columns):
        return [pltpu.VMEM((2, 4 * far_rows, columns), BF16), pltpu.SemaphoreType.DMA((2, 4))]

    early_far = far_blocks(early)
    early_one, early_two = near_step(early_far, 0), near_step(early_far, 1)
    crossing_far = far_blocks(tie(crossing, early_far))
    positions = count // size
    token_slices = lax.all_to_all(
        tie(tokens, early_far).reshape(size, positions, depth),
        "tm", split_axis=0, concat_axis=0, tiled=True,
    ).reshape(count, depth)
    ordered, wide, *ordered_others = call(
        functools.partial(order_kernel, others=len(others)),
        [shaped(count, depth), shaped(count, size * block)]
        + [shaped(count, depth) for _ in others],
        tokens, *others, source, wide_source,
        name="order", us=6,
    )

    early_near = early_far, early_one, early_two, near_step(tie(early_one, ordered), 1)
    wide_slices = call(
        functools.partial(widen_kernel, positions=positions),
        shaped(count, size * block), token_slices, wide_source, name="widen", us=2,
    )
    closing_far = far_blocks(tie(closing, token_slices))
    early_rows = early_far.shape[0]
    early = with_other_core(early_near)
    timed = call(
        functools.partial(time_kernel, positions=positions),
        shaped(count, 2 * tw),
        which, wide_slices,
        scalars=1,
        pieces=early,
        scratch=[pltpu.VMEM((2, count, tw), F32)]
        + weight_scratch(early_rows, whole_tiles(3 * tw)),
        name="timed", us=5,
    )
    timed_here = timed
    crossing = near_blocks(tie(crossing_far, early_one, early_two), timed_here)
    timed = lax.all_to_all(
        timed.reshape(size, positions, 2 * tw), "tm", split_axis=0, concat_axis=0, tiled=True
    ).reshape(count, 2 * tw)
    gates = box_gate.reshape(2, bw)
    gates = jnp.where(half == 0, gates, gates[::-1])
    boxed = call(
        functools.partial(box_kernel, slots=slots, blocks=size, skip=3 * tw),
        shaped(count, 2 * bw),
        which, wide, wide_source, gates,
        scalars=1,
        pieces=early,
        scratch=[
            pltpu.VMEM((count, bw), F32),
            pltpu.VMEM((size * slots, depth), F32),
            pltpu.VMEM((size, 128), F32),
            *weight_scratch(early_rows, width - 3 * tw // 128 * 128)[:1],
            pltpu.VMEM((size * block, width), BF16),
            *weight_scratch(early_rows, width)[1:],
            pltpu.SemaphoreType.DMA((4,)),
        ],
        name="boxed", us=7, vmem_mib=16 + size // 2,
    )
    closing = near_blocks(closing_far, timed_here)
    cross_rows = crossing[0].shape[0]
    cross = call(
        functools.partial(cross_kernel, others=len(others)),
        shaped(count, 2 * cw),
        which, tie(link_counts, timed_here), ordered, *ordered_others,
        scalars=2,
        pieces=with_other_core(crossing),
        scratch=[pltpu.VMEM((count, cw), F32)] + weight_scratch(cross_rows, cross_width),
        name="cross", us=9,
    )
    result = call(
        final_kernel, shaped(count, depth), which, tokens, source, cross, timed, boxed,
        scalars=1,
        pieces=with_other_core(closing),
        scratch=weight_scratch(closing[0].shape[0], out_width),
        name="final", us=5,
    )
    return result.reshape(frames_x.shape)


def solution(mesh):
    in_specs = (
        P("view", "tm", None, None),
        P("view", "tm", None, None),
        P("view", "tm"),
        P("view", "tm"),
        P("view", None),
        P("tm", None),
        P("tm", None),
        P(),
    )
    out_specs = P("view", "tm", None, None)
    return jax.shard_map(
        per_device, mesh=mesh, in_specs=in_specs, out_specs=out_specs, check_vma=False
    )
```

```python
import functools
import math

import jax
import jax.numpy as jnp
from jax import lax
from jax.experimental import pallas as pl
from jax.experimental.pallas import tpu as pltpu
from jax.sharding import PartitionSpec as P

HD = 72
CROSS_HEADS = 8
TIME_HEADS = 4
BOX_HEADS = 4
DEAD = -1e30
DEFINITE = 1e29
F32 = jnp.float32
BF16 = jnp.bfloat16
FLOPS_A_US = 1.1e9
BYTES_A_US = 3.6e6


def swap(value, axis, by):
    size = lax.axis_size(axis)
    return lax.ppermute(value, axis, [(i, i ^ by) for i in range(size)])


def tie(value, *before):
    return lax.optimization_barrier((value, *before))[0]


def far_blocks(shard):
    size = lax.axis_size("tm")
    parts = [swap(shard, "tm", d) for d in range(4, size, 4)]
    return jnp.concatenate([shard] + parts, axis=0)


def near_step(value, step):
    size, cameras = lax.axis_size("tm"), lax.axis_size("view")
    pairs = [
        (v * size + i, v * size + (i ^ (1 << (v + step) % 2)))
        for v in range(cameras)
        for i in range(size)
    ]
    return lax.ppermute(value, ("view", "tm"), pairs)


def load_blocks(pieces, first, scratch, sems, columns):
    rows = pieces[0].shape[0]
    to = [0, (1 + first) * rows, (2 - first) * rows, 3 * rows]
    copies = [
        pltpu.make_async_copy(
            piece.at[:, columns], scratch.at[pl.ds(pl.multiple_of(at, 16), rows)], sems.at[j]
        )
        for j, (piece, at) in enumerate(zip(pieces, to))
    ]
    for copy in copies:
        copy.start()

    def wait():
        for copy in copies:
            copy.wait()

    return wait


def block_order(size):
    far = list(range(0, size, 4))
    return [f ^ low for low in range(4) for f in far]


def dot(a, b):
    return jnp.dot(a, b, preferred_element_type=F32)


def dot_t(a, b):
    return lax.dot_general(a, b, (((1,), (1,)), ((), ())), preferred_element_type=F32)


def chooser(rows, source, offset=0):
    row_ids = lax.broadcasted_iota(jnp.int32, (rows, source.shape[1]), 0)
    return (row_ids + offset == source).astype(F32).astype(BF16)


def attend_heads(query, keys, values, masks, offsets, store):
    width = query.shape[1]
    scale = HD ** (-0.5) * math.log2(math.e)
    for head in range(width // HD):
        low, high = head * HD, (head + 1) * HD
        left = low // 128 * 128
        right = min(width, -(-high // 128) * 128)
        spare = right - 1 - left if high < right else 0
        lane = lax.broadcasted_iota(jnp.int32, (1, right - left), 1) + left
        mine = (lane >= low) & (lane < high)
        counts = lane == spare + left
        q = jnp.where(mine, query[:, left:right].astype(F32), 0.0).astype(BF16)
        scores = dot_t(q, jnp.concatenate([k[:, left:right] for k in keys], axis=0))
        ends = [0]
        for k in keys:
            ends.append(ends[-1] + k.shape[0])
        scores = [scores[:, a:b] for a, b in zip(ends[:-1], ends[1:])]
        scores = [s if m is None else jnp.where(m, s, DEAD) for s, m in zip(scores, masks)]
        tops = [
            functools.reduce(
                jnp.maximum, [s[:, at : at + 128] for at in range(0, s.shape[1], 128)]
            )
            for s in scores
        ]
        tops = [t if o is None else jnp.where(o < DEFINITE, t, DEAD) for t, o in zip(tops, offsets)]
        top = jnp.max(functools.reduce(jnp.maximum, tops), axis=-1, keepdims=True)
        expos = [
            jnp.exp2((s - (top if o is None else top + o)) * scale).astype(BF16)
            for s, o in zip(scores, offsets)
        ]
        value = jnp.concatenate([v[:, left:right] for v in values], axis=0)
        value = jnp.where(counts, 1.0, value.astype(F32)).astype(BF16)
        out = dot(jnp.concatenate(expos, axis=1), value)
        store(left, right, mine, out / out[:, spare : spare + 1])


def keep_rows(half, ref, at, end, left, right, mine, result):
    ref[half, at:end, left:right] = jnp.where(mine, result, ref[half, at:end, left:right])


def keep_in(ref):
    def store(left, right, mine, result):
        ref[:, left:right] = jnp.where(mine, result, ref[:, left:right])

    return store


def send_kernel(
    half_ref, count_ref, valid_ref, qkv_hbm, w_out_hbm, box_hbm, early_ref, cross_ref, closing_ref,
    qkv_ref, w_out_ref, box_ref, sems, *, parts,
):
    copies = [
        pltpu.make_async_copy(a, b, sems.at[j])
        for j, (a, b) in enumerate(
            ((qkv_hbm, qkv_ref), (box_hbm, box_ref), (w_out_hbm, w_out_ref))
        )
    ]
    for copy in copies:
        copy.start()
    for copy in copies:
        copy.wait()
    cw, tw, bw = parts
    block, width = early_ref.shape
    rows, depth = w_out_ref.shape
    lane = lax.broadcasted_iota(jnp.int32, (8, 128), 1)
    live = (lane < count_ref[0, 0]) & (lane < box_ref.shape[0])
    flags = jnp.where(live & (jnp.full((8, 128), valid_ref[0, 0]) == 1), 1.0, 0.0)
    boxes = box_ref[...].astype(F32)
    carried = [boxes[:8], boxes[8:], flags]
    filled = 2 * depth + 128
    carried = jnp.concatenate(carried + [jnp.zeros((8, 3 * width - filled), F32)], axis=1)
    carried = [carried[:, j * width : (j + 1) * width] for j in range(3)]

    def side_columns(side):
        def part(base, size):
            at = [kind * depth + base + side * size for kind in range(3)]
            return [qkv_ref[:, a : a + size].astype(F32) for a in at]

        def fill(x, to, axis):
            size = list(x.shape)
            size[axis] = to - size[axis]
            return jnp.concatenate([x, jnp.zeros(size, F32)], axis) if size[axis] else x

        weights = jnp.concatenate(part(2 * cw, tw) + part(2 * cw + 2 * tw, bw), axis=1)
        early = jnp.concatenate(carried + [fill(weights, width, 1)], axis=0)
        early_ref[...] = fill(early, block, 0).astype(BF16)
        cross = jnp.concatenate(part(0, cw), axis=1)
        cross_ref[...] = fill(cross, cross_ref.shape[1], 1).astype(BF16)
        at = side * (depth - closing_ref.shape[1])
        closing_ref[...] = w_out_ref[:, at : at + closing_ref.shape[1]]

    for side in range(2):
        pl.when(half_ref[0] == side)(functools.partial(side_columns, side))


def order_kernel(tokens_ref, *refs, others):
    other_refs = refs[:others]
    source_ref, wide_source_ref, out_ref, wide_ref = refs[others : others + 4]
    out_refs = refs[others + 4 :]
    depth = tokens_ref.shape[1]
    pick = chooser(depth, source_ref[...])
    out_ref[...] = dot(tokens_ref[...], pick).astype(BF16)
    for a, b in zip(other_refs, out_refs):
        b[...] = dot(a[...], pick).astype(BF16)
    wide_ref[...] = dot(tokens_ref[...], chooser(depth, wide_source_ref[...])).astype(BF16)


def regroup(rows, positions):
    frames = rows // positions
    to = lax.broadcasted_iota(jnp.int32, (rows, 1), 0)
    source = (to % frames) * positions + to // frames
    return (lax.broadcasted_iota(jnp.int32, (1, rows), 1) == source).astype(F32).astype(BF16)


def widen_kernel(tokens_ref, source_ref, wide_ref, *, positions):
    tokens = tokens_ref[...]
    tokens = dot(regroup(tokens.shape[0], positions), tokens).astype(BF16)
    wide_ref[...] = dot(tokens, chooser(tokens.shape[1], source_ref[...])).astype(BF16)


def load_halves(half_ref, piece_refs, scratch, sems, columns):
    return [
        load_blocks(
            piece_refs[4 * j : 4 * j + 4],
            half_ref[0] if j == 0 else 1 - half_ref[0],
            scratch.at[j],
            sems.at[j],
            columns,
        )
        for j in range(2)
    ]


def time_kernel(half_ref, wide_ref, *refs, positions):
    piece_refs, (out_ref, acc_ref, weight_ref, sems) = refs[:8], refs[8:]
    waits = load_halves(half_ref, piece_refs, weight_ref, sems, pl.ds(0, weight_ref.shape[2]))
    rows = wide_ref.shape[0]
    frames = rows // positions
    part = out_ref.shape[1] // 2
    step = max(frames, 128) if rows % max(frames, 128) == 0 else rows
    group = lax.broadcasted_iota(jnp.int32, (step, 1), 0) // frames
    group_t = lax.broadcasted_iota(jnp.int32, (1, step), 1) // frames
    live = group == group_t
    wide = wide_ref[...]
    for half in range(2):
        waits[half]()
        qkv = dot(wide, weight_ref[half]).astype(BF16)
        q, k, v = (qkv[:, j * part : (j + 1) * part] for j in range(3))
        for at in range(0, rows, step):
            end = at + step
            attend_heads(
                q[at:end], [k[at:end]], [v[at:end]], [live], [None],
                functools.partial(keep_rows, half, acc_ref, at, end),
            )
    timed = jnp.concatenate([acc_ref[0].astype(BF16), acc_ref[1].astype(BF16)], axis=1)
    back = lax.dot_general(
        regroup(rows, positions), timed, (((0,), (0,)), ((), ())), preferred_element_type=F32
    )
    out_ref[...] = back.astype(BF16)


def box_kernel(
    half_ref, wide_ref, source_ref, gate_ref, *refs, slots, blocks, skip
):
    piece_refs = refs[:8]
    out_ref, acc_ref, box_ref, flag_ref, weight_ref, carried_ref, sems, carried_sems = refs[8:]
    part = out_ref.shape[1] // 2
    depth = box_ref.shape[1]
    block, width = carried_ref.shape[0] // blocks, carried_ref.shape[1]
    left = skip // 128 * 128
    carried = load_blocks(
        piece_refs[:4], half_ref[0], carried_ref, carried_sems, pl.ds(0, width)
    )
    waits = load_halves(
        half_ref, piece_refs, weight_ref, sems, pl.ds(left, weight_ref.shape[2])
    )
    wide = wide_ref[...]
    shift = skip - left
    carried()
    for b in range(blocks):
        at = b * block
        top = carried_ref[at : at + 16, :].astype(F32)
        low = carried_ref[at + 16 : at + 32, :].astype(F32)[:8]
        spread = 2 * width - depth
        rest = depth - spread
        to = b * 8
        box_ref[to : to + 8, :width] = top[:8]
        box_ref[to : to + 8, width:] = top[8:, : depth - width]
        to += blocks * 8
        box_ref[to : to + 8, :spread] = top[8:, depth - width :]
        box_ref[to : to + 8, spread:] = low[:, :rest]
        flag_ref[b : b + 1, :] = low[:1, rest : rest + 128]
    slot_lane = lax.broadcasted_iota(jnp.int32, (1, blocks * slots), 1)
    group = slot_lane // (8 * blocks)
    slot = group * 8 + slot_lane % 8
    of_block = (slot_lane // 8) % blocks
    spread_slots = (
        lax.broadcasted_iota(jnp.int32, (128, blocks * slots), 0) == slot
    ).astype(F32)
    flags = dot(flag_ref[...].astype(BF16), spread_slots.astype(BF16))
    mine = lax.broadcasted_iota(jnp.int32, (blocks, blocks * slots), 0) == of_block
    live = jnp.sum(jnp.where(mine, flags, 0.0), axis=0, keepdims=True)
    box = dot(box_ref[...].astype(BF16), chooser(depth, source_ref[...])).astype(BF16)
    for half in range(2):
        waits[half]()
        weights = weight_ref[half]
        qkv = dot(wide, weights).astype(BF16)[:, shift : shift + 3 * part]
        box_kv = dot(box, weights).astype(BF16)[:, shift + part : shift + 3 * part]
        attend_heads(
            qkv[:, :part],
            [qkv[:, part : 2 * part], box_kv[:, :part]],
            [qkv[:, 2 * part :], box_kv[:, part:]],
            [None, live > 0],
            [None, None],
            keep_in(acc_ref),
        )
        out_ref[:, half * part : (half + 1) * part] = (
            acc_ref[...] * jnp.tanh(gate_ref[half : half + 1, :])
        ).astype(BF16)


def cross_kernel(half_ref, count_ref, tokens_ref, *refs, others):
    other_refs, piece_refs = refs[:others], refs[others : others + 8]
    out_ref, acc_ref, weight_ref, sems = refs[others + 8 :]
    waits = load_halves(half_ref, piece_refs, weight_ref, sems, pl.ds(0, weight_ref.shape[2]))
    part = out_ref.shape[1] // 2
    unit = math.log(2) / HD ** (-0.5)
    offsets = [None]
    for j in range(others):
        count = jnp.full((1, 1), count_ref[0, j], F32)
        offsets.append(jnp.where(count > 1.5, -unit, jnp.where(count > 0.5, 0.0, -DEAD)))
    for half in range(2):
        waits[half]()
        weights = weight_ref[half]
        own = dot(tokens_ref[...], weights).astype(BF16)
        at = part // 128 * 128
        kv = [own[:, part : 3 * part]] + [
            dot(o[...], weights[:, at:]).astype(BF16)[:, part - at : 3 * part - at]
            for o in other_refs
        ]
        attend_heads(
            own[:, :part],
            [x[:, :part] for x in kv],
            [x[:, part:] for x in kv],
            [None] * (1 + others),
            offsets,
            keep_in(acc_ref),
        )
        out_ref[:, half * part : (half + 1) * part] = acc_ref[...].astype(BF16)


def final_kernel(half_ref, tokens_ref, source_ref, cross_ref, time_ref, box_ref, *refs):
    piece_refs, (out_ref, weight_ref, sems) = refs[:8], refs[8:]
    width = weight_ref.shape[2]
    waits = load_halves(half_ref, piece_refs, weight_ref, sems, pl.ds(0, width))
    which = half_ref[0]
    attn = None
    base = 0
    for ref in (cross_ref, time_ref, box_ref):
        part = ref.shape[1] // 2
        row = lax.broadcasted_iota(jnp.int32, (2 * part, 1), 0)
        channel = base + row + jnp.where(row < part, which, -which) * part
        term = dot(ref[...], (channel == source_ref[...]).astype(F32).astype(BF16))
        attn = term if attn is None else attn + term
        base += 2 * part
    attn = attn.astype(BF16)
    step = out_ref.shape[1] - width
    for half in range(2):
        waits[half]()
        side = which if half == 0 else 1 - which
        at = pl.ds(pl.multiple_of(side * step, 128), width)
        out_ref[:, at] = (tokens_ref[:, at].astype(F32) + dot(attn, weight_ref[half])).astype(BF16)


def call(
    kernel, outs, *args, scalars=0, scratch=(), pieces=(), name=None, vmem_mib=24, us=4
):
    vmem = pl.BlockSpec(memory_space=pltpu.VMEM)
    smem = pl.BlockSpec(memory_space=pltpu.SMEM)
    hbm = pl.BlockSpec(memory_space=pltpu.HBM)
    single = not isinstance(outs, list)
    return pl.pallas_call(
        kernel,
        out_shape=outs if single else tuple(outs),
        in_specs=[smem] * scalars + [vmem] * (len(args) - scalars) + [hbm] * len(pieces),
        out_specs=vmem if single else tuple(vmem for _ in outs),
        scratch_shapes=list(scratch),
        compiler_params=pltpu.CompilerParams(vmem_limit_bytes=vmem_mib * 2**20),
        cost_estimate=pl.CostEstimate(
            flops=int(us * FLOPS_A_US), bytes_accessed=int(us * BYTES_A_US), transcendentals=0
        ),
        name=name,
    )(*args, *pieces)


def whole_tiles(width):
    return -(-width // 128) * 128


def shaped(*dims):
    return jax.ShapeDtypeStruct(dims, BF16)


def per_device(frames_x, box_embed, box_count, frame_valid, cycle_link, w_qkv, w_out, box_gate):
    size = lax.axis_size("tm")
    cameras = lax.axis_size("view")
    depth = frames_x.shape[3]
    tokens = frames_x.reshape(-1, depth)
    count = tokens.shape[0]
    slots = box_embed.shape[2]
    boxes = box_embed.reshape(slots, depth)
    rows = w_qkv.shape[0]
    index = lax.axis_index("tm")
    half = lax.axis_index("view") % 2
    cw, tw, bw = (heads * HD // 2 for heads in (CROSS_HEADS, TIME_HEADS, BOX_HEADS))

    width, out_width = whole_tiles(3 * (tw + bw)), whole_tiles(depth // 2)
    cross_width = whole_tiles(3 * cw)
    used = 24 + rows
    block = -(-used // 16) * 16
    which = half.reshape(1).astype(jnp.int32)
    early, crossing, closing = call(
        functools.partial(send_kernel, parts=(cw, tw, bw)),
        [shaped(block, width), shaped(rows, cross_width), shaped(rows, out_width)],
        which, box_count, frame_valid,
        scalars=3,
        pieces=(w_qkv, w_out, boxes),
        scratch=[pltpu.VMEM(x.shape, BF16) for x in (w_qkv, w_out, boxes)]
        + [pltpu.SemaphoreType.DMA((3,))],
        name="send", us=2,
    )

    if cameras == 2:
        others = [swap(tokens, "view", 1)]
        link_counts = (cycle_link[:, :1] + cycle_link[:, 1:]).astype(F32)
    else:
        ring = range(cameras)
        others = [
            lax.ppermute(tokens, "view", [(i, (i + by) % cameras) for i in ring]) for by in (1, -1)
        ]
        link_counts = cycle_link.astype(F32)
    owners = index ^ jnp.array(block_order(size), jnp.int32)
    source = (owners[:, None] * rows + jnp.arange(rows)[None]).reshape(1, -1)
    wide_source = jnp.full((size, block), -1, jnp.int32)
    wide_source = wide_source.at[:, 24:used].set(source.reshape(size, rows)).reshape(1, -1)

    def near_blocks(far, *before):
        one = near_step(far, 0)
        two = near_step(far, 1)
        return far, one, two, near_step(tie(one, *before), 1)

    def with_other_core(blocks):
        return (*blocks, *(swap(b, "view", 1) for b in blocks))

    def weight_scratch(far_rows, columns):
        return [pltpu.VMEM((2, 4 * far_rows, columns), BF16), pltpu.SemaphoreType.DMA((2, 4))]

    early_far = far_blocks(early)
    early_one, early_two = near_step(early_far, 0), near_step(early_far, 1)
    crossing_far = far_blocks(tie(crossing, early_far))
    positions = count // size
    token_slices = lax.all_to_all(
        tie(tokens, early_far).reshape(size, positions, depth),
        "tm", split_axis=0, concat_axis=0, tiled=True,
    ).reshape(count, depth)
    ordered, wide, *ordered_others = call(
        functools.partial(order_kernel, others=len(others)),
        [shaped(count, depth), shaped(count, size * block)]
        + [shaped(count, depth) for _ in others],
        tokens, *others, source, wide_source,
        name="order", us=6,
    )

    early_near = early_far, early_one, early_two, near_step(tie(early_one, ordered), 1)
    wide_slices = call(
        functools.partial(widen_kernel, positions=positions),
        shaped(count, size * block), token_slices, wide_source, name="widen", us=2,
    )
    closing_far = far_blocks(tie(closing, token_slices))
    early_rows = early_far.shape[0]
    early = with_other_core(early_near)
    timed = call(
        functools.partial(time_kernel, positions=positions),
        shaped(count, 2 * tw),
        which, wide_slices,
        scalars=1,
        pieces=early,
        scratch=[pltpu.VMEM((2, count, tw), F32)]
        + weight_scratch(early_rows, whole_tiles(3 * tw)),
        name="timed", us=5,
    )
    timed_here = timed
    crossing = near_blocks(tie(crossing_far, early_one, early_two), timed_here)
    timed = lax.all_to_all(
        timed.reshape(size, positions, 2 * tw), "tm", split_axis=0, concat_axis=0, tiled=True
    ).reshape(count, 2 * tw)
    gates = box_gate.reshape(2, bw)
    gates = jnp.where(half == 0, gates, gates[::-1])
    boxed = call(
        functools.partial(box_kernel, slots=slots, blocks=size, skip=3 * tw),
        shaped(count, 2 * bw),
        which, wide, wide_source, gates,
        scalars=1,
        pieces=early,
        scratch=[
            pltpu.VMEM((count, bw), F32),
            pltpu.VMEM((size * slots, depth), F32),
            pltpu.VMEM((size, 128), F32),
            *weight_scratch(early_rows, width - 3 * tw // 128 * 128)[:1],
            pltpu.VMEM((size * block, width), BF16),
            *weight_scratch(early_rows, width)[1:],
            pltpu.SemaphoreType.DMA((4,)),
        ],
        name="boxed", us=7, vmem_mib=16 + size // 2,
    )
    closing = near_blocks(closing_far, timed_here)
    cross_rows = crossing[0].shape[0]
    cross = call(
        functools.partial(cross_kernel, others=len(others)),
        shaped(count, 2 * cw),
        which, tie(link_counts, timed_here), ordered, *ordered_others,
        scalars=2,
        pieces=with_other_core(crossing),
        scratch=[pltpu.VMEM((count, cw), F32)] + weight_scratch(cross_rows, cross_width),
        name="cross", us=9,
    )
    result = call(
        final_kernel, shaped(count, depth), which, tokens, source, cross, timed, boxed,
        scalars=1,
        pieces=with_other_core(closing),
        scratch=weight_scratch(closing[0].shape[0], out_width),
        name="final", us=5,
    )
    return result.reshape(frames_x.shape)


def solution(mesh):
    in_specs = (
        P("view", "tm", None, None),
        P("view", "tm", None, None),
        P("view", "tm"),
        P("view", "tm"),
        P("view", None),
        P("tm", None),
        P("tm", None),
        P(),
    )
    out_specs = P("view", "tm", None, None)
    return jax.shard_map(
        per_device, mesh=mesh, in_specs=in_specs, out_specs=out_specs, check_vma=False
    )
```
